32 devices in a mesh: groups: 2 (over x), vocab: 8 (over z, y), tokens: 2 (over core).
Axes of the slice: x: 2, y: 2, z: 4, core: 2. Of those that a mesh axis runs over, the one named last changes fastest.
Arguments:
- teacher_hidden: bfloat16 [2048, 4608], P(('groups', 'vocab', 'tokens')), parts along dimension 0, may hold values from -24 to 24
- route: int32 [32], P('groups'), parts along dimension 0, may hold values from 0 to 15, each once
- teacher_head: bfloat16 [4608, 16000], P('tokens', 'vocab'), may hold values from -0.09375 to 0.09375
- student_logits: bfloat16 [2048, 16000], P(('groups', 'tokens'), 'vocab'), parts along dimension 0, may hold values from -40 to 40
- targets: int32 [2048], P(('groups', 'tokens')), parts along dimension 0, may hold values from 0 to 15999
Outputs:
- gradient: bfloat16 [2048, 16000], P(('groups', 'tokens'), 'vocab'), parts along dimension 0
- token_loss: float32 [2048], P(('groups', 'tokens')), parts along dimension 0
The draws below stay inside these ranges and needn't reach their ends.
There are 2 independent parts, one for each index of `groups`. The reference program is written for one: setup_inputs(seed, part) draws one part's arguments, and reference() takes and returns one part's arrays. A program takes and returns all parts, laid end to end along the dimension named above; an argument that names none is the same for every part. Nothing has to cross between parts.
Inputs may be any that keep to these rules, and one draw needn't show every extreme that they name: route is a permutation of 0 to 15.
All inputs are finite; a program needn't handle non-finite values.
Results may differ from the reference program's by a relative error of at most 0.001.
Values may be sent and summed in bfloat16 or wider, within the bound.
A program may use at most 64 MiB of HBM per device.

```python
import math
import jax
import jax.numpy as jnp
import numpy as np
from jax import lax

DT = 4608
BLOCK_ROWS = 64
VOCAB = 16000
TOKENS = 1024
NBLOCK = 16


def draw_student_logits(key, part):
    key = jax.random.fold_in(key, 11)
    noise_key, column_key, row_key = jax.random.split(key, 3)
    position = jnp.arange(VOCAB, dtype=jnp.float32)[None, :] / VOCAB
    column_scale = jnp.exp(jax.random.uniform(column_key, (1, VOCAB), jnp.float32, jnp.log(1.5), jnp.log(5.0)))
    noise = jax.random.normal(noise_key, (TOKENS, VOCAB), jnp.float32)
    row_scale = jnp.exp(jax.random.uniform(row_key, (TOKENS, 1), jnp.float32, jnp.log(0.7), jnp.log(1.4)))
    values = 1.2 * position + row_scale * column_scale * noise
    return jnp.clip(values, -40.0, 40.0).astype(jnp.bfloat16)


def place_ends(result, key, low, high):
    shape = result.shape
    place = [jax.random.randint(jax.random.fold_in(key, axis), (), 0, shape[axis]) for axis in range(len(shape))]
    result = result.at[tuple(place)].set(low)
    longest = shape.index(max(shape))
    place[longest] = (place[longest] + 1) % shape[longest]
    return result.at[tuple(place)].set(high)


def block_scale(own_key, shape, cuts, least, high):
    gain = 1.0
    for axis_at, parts in cuts:
        steps = jax.random.uniform(jax.random.fold_in(jax.random.fold_in(own_key, 6), axis_at), (parts,), jnp.float32, least / len(cuts), high / len(cuts))
        gain = gain * jnp.repeat(jnp.exp(steps), shape[axis_at] // parts).reshape((-1,) + (1,) * (len(shape) - 1 - axis_at))
    return gain


def rank_bounds(amount, lean):
    weights = [(1 << 20) // math.isqrt(standing ** lean) + 1 for standing in range(1, amount + 1)]
    width = 1 + sum(weights) // (1 << 30)
    return np.cumsum(np.array([max(1, weight // width) for weight in weights]))


def ranked_ids(key, shape, number_of, lean):
    listing = rank_bounds(number_of, lean)
    ticket = jax.random.randint(jax.random.fold_in(key, 1), shape, 0, int(listing[number_of - 1]))
    standing = jnp.searchsorted(jnp.asarray(listing, jnp.int32), ticket, side="right")
    return jax.random.permutation(jax.random.fold_in(key, 2), number_of)[standing].astype(jnp.int32)


def gaussian(own_key, extent, scale, most, cuts=(), kind=jnp.bfloat16):
    values = scale * jax.random.normal(own_key, extent, jnp.float32)
    if cuts:
        values = values * block_scale(own_key, extent, cuts, -0.22, 0.18)
    return jnp.clip(values, -most, most).astype(kind)


def setup_inputs(seed: int = 0, part: int = 0) -> dict:
    keys = jax.random.split(jax.random.key(seed), 6)
    own_keys = jax.random.split(jax.random.fold_in(keys[5], part), 6)
    teacher_hidden = gaussian(own_keys[0], (TOKENS, DT), 4.0, 24.0, ((0, 16),))
    route = jax.random.permutation(own_keys[1], NBLOCK).astype(jnp.int32)
    teacher_head = gaussian(keys[2], (DT, VOCAB), DT ** -0.5, 0.09375, ((0, 2), (1, 8)))
    student_logits = draw_student_logits(jax.random.fold_in(jax.random.fold_in(keys[5], part), 71), part)
    targets = place_ends(ranked_ids(own_keys[4], (TOKENS,), VOCAB, 2), jax.random.fold_in(own_keys[4], 3), 0, VOCAB - 1).astype(jnp.int32)
    return dict(teacher_hidden=teacher_hidden, route=route, teacher_head=teacher_head, student_logits=student_logits, targets=targets)


SOFT_CAP = 30.0
MIX_WEIGHT = 0.5


def capped_of(values):
    return SOFT_CAP * jnp.tanh(values / SOFT_CAP)


def reference(teacher_hidden, route, teacher_head, student_logits, targets):
    blocks = teacher_hidden.reshape(NBLOCK, BLOCK_ROWS, DT)
    aligned = jnp.take(blocks, route.astype(jnp.int32), axis=0)
    student_blocks = student_logits.reshape(NBLOCK, BLOCK_ROWS, VOCAB)
    target_blocks = targets.reshape(NBLOCK, BLOCK_ROWS)

    def one_block(members):
        teacher_rows, raw_logits, block_targets = members
        teacher_capped = capped_of(jnp.dot(teacher_rows, teacher_head, preferred_element_type=jnp.float32))
        capped = capped_of(raw_logits.astype(jnp.float32))
        exp_teacher = jnp.exp(teacher_capped)
        exp_student = jnp.exp(capped)
        teacher_total = jnp.sum(exp_teacher, axis=1)
        student_total = jnp.sum(exp_student, axis=1)
        cross_sum = jnp.sum(exp_teacher * (teacher_capped - capped), axis=1)
        target_hits = jnp.arange(VOCAB, dtype=jnp.int32)[None, :] == block_targets[:, None]
        picked = jnp.sum(jnp.where(target_hits, capped, jnp.zeros_like(capped)), axis=1)
        log_student = jnp.log(student_total)
        token_loss = MIX_WEIGHT * (cross_sum / teacher_total - jnp.log(teacher_total) + log_student) + (1.0 - MIX_WEIGHT) * (log_student - picked)
        cap_slope = 1.0 - (capped / SOFT_CAP) ** 2
        gradient = (exp_student / student_total[:, None] - MIX_WEIGHT * exp_teacher / teacher_total[:, None] - (1.0 - MIX_WEIGHT) * target_hits.astype(jnp.float32)) * cap_slope
        return gradient.astype(jnp.bfloat16), token_loss

    gradients, losses = lax.map(one_block, (aligned, student_blocks, target_blocks))
    return gradients.reshape(TOKENS, VOCAB), losses.reshape(TOKENS)
```

```python
import jax
import jax.numpy as jnp
from jax import lax
from jax.experimental import pallas as pl
from jax.experimental.pallas import tpu as pltpu
from jax.sharding import PartitionSpec as P

BLOCK_ROWS = 64


SOFT_CAP = 30.0
MIX_WEIGHT = 0.5


def from_partner(value, axis, bit):
    mask = 2**bit
    pairs = [(source, source ^ mask) for source in range(lax.axis_size(axis))]
    return lax.ppermute(value, axis, pairs)


def capped_of(values):
    return SOFT_CAP * jnp.tanh(values / SOFT_CAP)


def logit_terms(features, weights):
    return jnp.dot(features, weights, preferred_element_type=jnp.float32)


def per_device(teacher_hidden, route, teacher_head, student_logits, targets):
    row_count, col_count = student_logits.shape
    head_rows = teacher_head.shape[0]
    token_index = lax.axis_index("tokens")
    vocab_index = lax.axis_index("vocab")
    capped = capped_of(student_logits.astype(jnp.float32))
    exp_student = jnp.exp(capped)
    columns = vocab_index * col_count + lax.broadcasted_iota(jnp.int32, (1, col_count), 1)
    target_hits = targets[:, None] == columns
    picked_part = jnp.sum(jnp.where(target_hits, capped, 0.0), axis=1)
    student_part = jnp.sum(exp_student, axis=1)
    own_half = lax.dynamic_slice_in_dim(teacher_hidden, token_index * head_rows, head_rows, 1)
    given_half = lax.dynamic_slice_in_dim(
        teacher_hidden, (1 - token_index) * head_rows, head_rows, 1
    )
    received = from_partner(given_half, "tokens", 0)
    lower_rows = jnp.where(token_index == 0, own_half, received)
    upper_rows = jnp.where(token_index == 0, received, own_half)
    paired = jnp.concatenate((lower_rows, upper_rows), axis=0)
    sliced = lax.all_gather(paired, "vocab", axis=0, tiled=True)
    half_blocks = sliced.reshape(-1, BLOCK_ROWS, head_rows)
    features = jnp.take(half_blocks, route, axis=0).reshape(-1, head_rows)
    teacher_raw = lax.psum_scatter(
        logit_terms(features, teacher_head), "tokens", scatter_dimension=0, tiled=True
    )
    teacher_capped = capped_of(teacher_raw)
    exp_teacher = jnp.exp(teacher_capped)
    teacher_part = jnp.sum(exp_teacher, axis=1)
    cross_part = jnp.sum(exp_teacher * (teacher_capped - capped), axis=1)
    student_total, picked, teacher_total, cross_sum = lax.psum(
        (student_part, picked_part, teacher_part, cross_part), "vocab"
    )
    log_student = jnp.log(student_total)
    token_loss = MIX_WEIGHT * (cross_sum / teacher_total - jnp.log(teacher_total) + log_student) + (
        1.0 - MIX_WEIGHT
    ) * (log_student - picked)
    cap_slope = 1.0 - (capped / SOFT_CAP) ** 2
    gradient = (
        exp_student / student_total[:, None]
        - MIX_WEIGHT * exp_teacher / teacher_total[:, None]
        - (1.0 - MIX_WEIGHT) * target_hits.astype(jnp.float32)
    ) * cap_slope
    return (gradient.astype(jnp.bfloat16), token_loss)


MESH = pl.DeviceIdType.MESH
ROWS = 16
LINE = 4
COLUMN_TILE = 512


def fused_kernel(
    hidden, route, head, student, targets,
    gradient, loss,
    head_v, feats, own_p, other_p, student_v, capped_v, exp_t, grad_v, target_v,
    stat, stat_all, stat_cols,
    load_sem, send_sem, recv_sem, part_send, part_recv, stat_send, stat_recv, store_sem,
):
    c = lax.axis_index("tokens")
    v = lax.axis_index("vocab")
    z = v // 2
    y = v - 2 * z
    unit = hidden.shape[0]
    depth = head.shape[0]
    cols = head.shape[1]
    token_rows = student.shape[0]
    peers = 2 * LINE
    partner = {"vocab": v, "tokens": 1 - c}

    def slot_of(zs, ys, s):
        return (zs * 2 + ys) * 2 + (c + s - 2 * c * s)

    def rows_of(slot):
        return pl.ds(pl.multiple_of(slot * unit, unit), unit)

    def half(which):
        return pl.ds(pl.multiple_of(which * depth, 128), depth)

    own_slot = slot_of(z, y, 0)
    load_own = pltpu.make_async_copy(hidden.at[:, half(c)], feats.at[rows_of(own_slot)], load_sem.at[0])
    load_head = pltpu.make_async_copy(head, head_v, load_sem.at[1])
    load_student = pltpu.make_async_copy(student, student_v, load_sem.at[2])
    load_target = pltpu.make_async_copy(targets, target_v, load_sem.at[3])
    load_own.start()

    barrier = pltpu.get_barrier_semaphore()
    pl.semaphore_signal(barrier, inc=1, device_id=partner, device_id_type=MESH)
    for d in range(1, peers):
        peer = {"vocab": lax.rem(v + d, peers), "tokens": c}
        pl.semaphore_signal(barrier, inc=1, device_id=peer, device_id_type=MESH)
    pl.semaphore_wait(barrier, peers)

    def partner_copy():
        return pltpu.make_async_remote_copy(
            src_ref=hidden.at[:, half(1 - c)],
            dst_ref=feats.at[rows_of(own_slot)],
            send_sem=send_sem.at[3, own_slot],
            recv_sem=recv_sem.at[own_slot],
            device_id=partner,
            device_id_type=MESH,
        )

    def unit_copy(way, slot):
        target = (v + 2, v - 2, v + 1 - 2 * y)[way]
        return pltpu.make_async_remote_copy(
            src_ref=feats.at[rows_of(slot)],
            dst_ref=feats.at[rows_of(slot)],
            send_sem=send_sem.at[way, slot],
            recv_sem=recv_sem.at[slot],
            device_id={"vocab": target, "tokens": c},
            device_id_type=MESH,
        )

    def arrived(slot):
        unit_copy(2, slot).wait_recv()

    def send_line(way, slot):
        @pl.when(z < LINE - 1 if way == 0 else z > 0)
        def _():
            unit_copy(way, slot).start()

    def part_copy(block):
        rows = pl.ds(2 * block, 2)
        return pltpu.make_async_remote_copy(
            src_ref=own_p.at[rows],
            dst_ref=other_p.at[rows],
            send_sem=part_send.at[block],
            recv_sem=part_recv.at[block],
            device_id=partner,
            device_id_type=MESH,
        )

    def multiply(block):
        rows = pl.ds(pl.multiple_of(block * 2 * unit, 2 * unit), 2 * unit)
        for first in range(0, cols, COLUMN_TILE):
            width = min(COLUMN_TILE, cols - first)
            own_p[pl.ds(2 * block, 2), :, first : first + width] = jnp.dot(
                feats[rows, :], head_v[:, first : first + width], preferred_element_type=jnp.float32
            ).reshape(2, unit, width)
        part_copy(block).start()

    partner_copy().start()
    load_own.wait()
    send_line(0, own_slot)
    send_line(1, own_slot)
    unit_copy(2, own_slot).start()
    load_head.start()
    load_student.start()
    load_target.start()
    own_second = slot_of(z, y, 1)
    arrived(own_second)
    send_line(0, own_second)
    send_line(1, own_second)
    unit_copy(2, own_second).start()

    load_student.wait()
    load_target.wait()
    columns = v * cols + lax.broadcasted_iota(jnp.int32, (1, cols), 1)
    lane = lax.broadcasted_iota(jnp.int32, (ROWS, 128), 1)

    def student_pass(i, carry):
        rows = pl.ds(pl.multiple_of(i * ROWS, ROWS), ROWS)
        capped = capped_of(student_v[rows, :].astype(jnp.float32))
        capped_v[rows, :] = capped
        total = jnp.sum(jnp.exp(capped), axis=1, keepdims=True)
        picked = jnp.sum(jnp.where(target_v[rows, :] == columns, capped, 0.0), axis=1, keepdims=True)
        stat_cols[rows, :] = jnp.where(lane == 0, total, jnp.where(lane == 1, picked, 0.0))
        return carry

    passes = token_rows // ROWS
    load_head.wait()
    multiply(v)

    def step(k, carry):
        for s in range(2):
            src = z - 1 - k

            @pl.when(src >= 0)
            def _():
                slot = slot_of(src, y, s)
                arrived(slot)
                send_line(0, slot)

                @pl.when((src > 0) if s else (src >= 0))
                def _():
                    unit_copy(2, slot).start()

            src_up = z + 1 + k

            @pl.when(src_up <= LINE - 1)
            def _():
                slot = slot_of(src_up, y, s)
                arrived(slot)
                send_line(1, slot)

                @pl.when((src_up < LINE - 1) if s else (src_up <= LINE - 1))
                def _():
                    unit_copy(2, slot).start()

            if s == 0:
                @pl.when((z == k) & (z > 0))
                def _():
                    slot = slot_of(0, 1 - y, 1)
                    arrived(slot)
                    send_line(0, slot)

                @pl.when((LINE - 1 - z == k) & (z < LINE - 1))
                def _():
                    slot = slot_of(LINE - 1, 1 - y, 1)
                    arrived(slot)
                    send_line(1, slot)

            across = z - k

            @pl.when((across >= 0) & ((s == 0) | (across > 0) | (k == 0)))
            def _():
                slot = slot_of(across, 1 - y, s)
                arrived(slot)
                if s == 1:
                    @pl.when((k == 0) & (z == 0))
                    def _():
                        unit_copy(0, slot).start()

                    @pl.when((k == 0) & (z == LINE - 1))
                    def _():
                        unit_copy(1, slot).start()

            across_up = z + k

            @pl.when((k > 0) & (across_up <= LINE - 1) & ((s == 0) | (across_up < LINE - 1)))
            def _():
                arrived(slot_of(across_up, 1 - y, s))

        def products(which, inner):
            zs = jnp.where(which == 0, z - 1 - k, jnp.where(which == 1, z + 1 + k, jnp.where(which == 2, z - k, z + k)))
            ys = jnp.where(which < 2, y, 1 - y)

            @pl.when((zs >= 0) & (zs <= LINE - 1) & ((which < 3) | (k > 0)))
            def _():
                multiply(zs * 2 + ys)

            return inner

        lax.fori_loop(0, 4, products, 0)

        @pl.when(k < LINE - 1)
        def _():
            lax.fori_loop(k * passes // (LINE - 1), (k + 1) * passes // (LINE - 1), student_pass, 0)

        return carry

    lax.fori_loop(0, LINE, step, 0)

    def await_part(block, carry):
        part_copy(block).wait_recv()
        return carry

    lax.fori_loop(0, peers, await_part, 0)

    per_block = BLOCK_ROWS // ROWS
    first_block = c * (token_rows // BLOCK_ROWS)

    def teacher_pass(i, carry):
        block = i // per_block
        inside = i - block * per_block
        rows = pl.ds(pl.multiple_of(i * ROWS, ROWS), ROWS)
        source = route[first_block + block]
        within = pl.ds(pl.multiple_of(inside * ROWS, ROWS), ROWS)
        teacher = capped_of(own_p[source, within, :] + other_p[source, within, :])
        grown = jnp.exp(teacher)
        exp_t[rows, :] = grown
        total = jnp.sum(grown, axis=1, keepdims=True)
        cross = jnp.sum(grown * (teacher - capped_v[rows, :]), axis=1, keepdims=True)
        before = stat_cols[rows, :]
        stat_cols[rows, :] = jnp.where(lane == 2, total, jnp.where(lane == 3, cross, before))
        return carry

    lax.fori_loop(0, passes, teacher_pass, 0)
    stat[...] = jnp.transpose(stat_cols[...])[0:8, :]

    def stat_copy(peer, slot):
        return pltpu.make_async_remote_copy(
            src_ref=stat,
            dst_ref=stat_all.at[slot],
            send_sem=stat_send.at[peer],
            recv_sem=stat_recv.at[slot],
            device_id={"vocab": peer, "tokens": c},
            device_id_type=MESH,
        )

    for d in range(1, peers):
        stat_copy(lax.rem(v + d, peers), v).start()
    stat_all[v] = stat[...]
    for d in range(1, peers):
        stat_copy(0, lax.rem(v + d, peers)).wait_recv()
    sums = stat_all[0]
    for d in range(1, peers):
        sums = sums + stat_all[d]
    log_student = jnp.log(sums[0:1, :])
    loss[...] = MIX_WEIGHT * (sums[3:4, :] / sums[2:3, :] - jnp.log(sums[2:3, :]) + log_student) + (
        1.0 - MIX_WEIGHT
    ) * (log_student - sums[1:2, :])
    scales = jnp.concatenate([1.0 / sums[0:1, :], MIX_WEIGHT / sums[2:3, :]], axis=0)
    scales = jnp.concatenate([scales, jnp.zeros((126, token_rows), jnp.float32)], axis=0)
    stat_cols[...] = jnp.transpose(scales)

    def gradient_pass(i, carry):
        rows = pl.ds(pl.multiple_of(i * ROWS, ROWS), ROWS)
        capped = capped_v[rows, :]
        hits = jnp.where(target_v[rows, :] == columns, 1.0 - MIX_WEIGHT, 0.0)
        scale = stat_cols[rows, :]
        value = jnp.exp(capped) * scale[:, 0:1] - exp_t[rows, :] * scale[:, 1:2] - hits
        slope = 1.0 - (capped / SOFT_CAP) ** 2
        grad_v[rows, :] = (value * slope).astype(grad_v.dtype)
        return carry

    pieces = 4
    piece_rows = token_rows // pieces
    for p in range(pieces):
        lax.fori_loop(p * passes // pieces, (p + 1) * passes // pieces, gradient_pass, 0)
        rows = pl.ds(p * piece_rows, piece_rows)
        pltpu.make_async_copy(grad_v.at[rows], gradient.at[rows], store_sem.at[p]).start()

    partner_copy().wait_send()
    for s in range(2):
        def sent(zs, carry):
            slot = slot_of(zs, y, s)

            @pl.when((z < LINE - 1) & (zs <= z))
            def _():
                unit_copy(0, slot).wait_send()

            @pl.when((z > 0) & (zs >= z))
            def _():
                unit_copy(1, slot).wait_send()

            @pl.when((zs == z) | (s == 0) | ((zs > 0) & (zs < LINE - 1)))
            def _():
                unit_copy(2, slot).wait_send()

            return carry

        lax.fori_loop(0, LINE, sent, 0)

    @pl.when(z < LINE - 1)
    def _():
        unit_copy(0, slot_of(0, 1 - y, 1)).wait_send()

    @pl.when(z > 0)
    def _():
        unit_copy(1, slot_of(LINE - 1, 1 - y, 1)).wait_send()

    def sent_part(block, carry):
        part_copy(block).wait_send()
        return carry

    lax.fori_loop(0, peers, sent_part, 0)
    for d in range(1, peers):
        stat_copy(lax.rem(v + d, peers), v).wait_send()
    for p in range(pieces):
        rows = pl.ds(p * piece_rows, piece_rows)
        pltpu.make_async_copy(grad_v.at[rows], gradient.at[rows], store_sem.at[p]).wait()


def fused(teacher_hidden, route, teacher_head, student_logits, targets):
    tokens, cols = student_logits.shape
    depth = teacher_head.shape[0]
    unit = teacher_hidden.shape[0]
    units = 4 * LINE
    anywhere = pl.BlockSpec(memory_space=pl.ANY)
    dma = pltpu.SemaphoreType.DMA
    gradient, loss = pl.pallas_call(
        fused_kernel,
        out_shape=(
            jax.ShapeDtypeStruct((tokens, cols), jnp.bfloat16),
            jax.ShapeDtypeStruct((1, tokens), jnp.float32),
        ),
        in_specs=[anywhere, pl.BlockSpec(memory_space=pltpu.SMEM), anywhere, anywhere, anywhere],
        out_specs=(anywhere, pl.BlockSpec(memory_space=pltpu.VMEM)),
        scratch_shapes=[
            pltpu.VMEM((depth, cols), jnp.bfloat16),
            pltpu.VMEM((units * unit, depth), jnp.bfloat16),
            pltpu.VMEM((units, unit, cols), jnp.float32),
            pltpu.VMEM((units, unit, cols), jnp.float32),
            pltpu.VMEM((tokens, cols), jnp.bfloat16),
            pltpu.VMEM((tokens, cols), jnp.float32),
            pltpu.VMEM((tokens, cols), jnp.float32),
            pltpu.VMEM((tokens, cols), jnp.bfloat16),
            pltpu.VMEM((tokens, 1), jnp.int32),
            pltpu.VMEM((8, tokens), jnp.float32),
            pltpu.VMEM((2 * LINE, 8, tokens), jnp.float32),
            pltpu.VMEM((tokens, 128), jnp.float32),
            dma((4,)),
            dma((4, units)),
            dma((units,)),
            dma((2 * LINE,)),
            dma((2 * LINE,)),
            dma((2 * LINE,)),
            dma((2 * LINE,)),
            dma((4,)),
        ],
        compiler_params=pltpu.CompilerParams(
            collective_id=0, has_side_effects=True, vmem_limit_bytes=56 * 2**20
        ),
    )(teacher_hidden, route, teacher_head, student_logits, targets[:, None])
    return gradient, loss.reshape(tokens)


def solution(mesh):
    body = fused if mesh.shape["vocab"] == 2 * LINE else per_device
    return jax.shard_map(
        body,
        mesh=mesh,
        in_specs=(
            P(("groups", "vocab", "tokens"), None),
            P("groups"),
            P("tokens", "vocab"),
            P(("groups", "tokens"), "vocab"),
            P(("groups", "tokens")),
        ),
        out_specs=(P(("groups", "tokens"), "vocab"), P(("groups", "tokens"))),
        check_vma=False,
    )
```

```python
import jax
import jax.numpy as jnp
from jax import lax
from jax.experimental import pallas as pl
from jax.experimental.pallas import tpu as pltpu
from jax.sharding import PartitionSpec as P

BLOCK_ROWS = 64


SOFT_CAP = 30.0
MIX_WEIGHT = 0.5


def from_partner(value, axis, bit):
    mask = 2**bit
    pairs = [(source, source ^ mask) for source in range(lax.axis_size(axis))]
    return lax.ppermute(value, axis, pairs)


def capped_of(values):
    return SOFT_CAP * jnp.tanh(values / SOFT_CAP)


def logit_terms(features, weights):
    return jnp.dot(features, weights, preferred_element_type=jnp.float32)


def per_device(teacher_hidden, route, teacher_head, student_logits, targets):
    row_count, col_count = student_logits.shape
    head_rows = teacher_head.shape[0]
    token_index = lax.axis_index("tokens")
    vocab_index = lax.axis_index("vocab")
    capped = capped_of(student_logits.astype(jnp.float32))
    exp_student = jnp.exp(capped)
    columns = vocab_index * col_count + lax.broadcasted_iota(jnp.int32, (1, col_count), 1)
    target_hits = targets[:, None] == columns
    picked_part = jnp.sum(jnp.where(target_hits, capped, 0.0), axis=1)
    student_part = jnp.sum(exp_student, axis=1)
    own_half = lax.dynamic_slice_in_dim(teacher_hidden, token_index * head_rows, head_rows, 1)
    given_half = lax.dynamic_slice_in_dim(
        teacher_hidden, (1 - token_index) * head_rows, head_rows, 1
    )
    received = from_partner(given_half, "tokens", 0)
    lower_rows = jnp.where(token_index == 0, own_half, received)
    upper_rows = jnp.where(token_index == 0, received, own_half)
    paired = jnp.concatenate((lower_rows, upper_rows), axis=0)
    sliced = lax.all_gather(paired, "vocab", axis=0, tiled=True)
    half_blocks = sliced.reshape(-1, BLOCK_ROWS, head_rows)
    features = jnp.take(half_blocks, route, axis=0).reshape(-1, head_rows)
    teacher_raw = lax.psum_scatter(
        logit_terms(features, teacher_head), "tokens", scatter_dimension=0, tiled=True
    )
    teacher_capped = capped_of(teacher_raw)
    exp_teacher = jnp.exp(teacher_capped)
    teacher_part = jnp.sum(exp_teacher, axis=1)
    cross_part = jnp.sum(exp_teacher * (teacher_capped - capped), axis=1)
    student_total, picked, teacher_total, cross_sum = lax.psum(
        (student_part, picked_part, teacher_part, cross_part), "vocab"
    )
    log_student = jnp.log(student_total)
    token_loss = MIX_WEIGHT * (cross_sum / teacher_total - jnp.log(teacher_total) + log_student) + (
        1.0 - MIX_WEIGHT
    ) * (log_student - picked)
    cap_slope = 1.0 - (capped / SOFT_CAP) ** 2
    gradient = (
        exp_student / student_total[:, None]
        - MIX_WEIGHT * exp_teacher / teacher_total[:, None]
        - (1.0 - MIX_WEIGHT) * target_hits.astype(jnp.float32)
    ) * cap_slope
    return (gradient.astype(jnp.bfloat16), token_loss)


MESH = pl.DeviceIdType.MESH
ROWS = 80
LINE = 4
COLUMN_TILE = 400


def fused_kernel(
    hidden, route, head, student, targets,
    gradient, loss,
    head_v, feats, own_p, other_p, student_v, capped_v, exp_s, exp_t, grad_v, target_v,
    stat, stat_all, sums_v,
    load_sem, send_sem, recv_sem, part_send, part_recv, stat_send, stat_recv, store_sem,
):
    c = lax.axis_index("tokens")
    v = lax.axis_index("vocab")
    z = v // 2
    y = v - 2 * z
    unit = hidden.shape[0]
    cols, depth = head.shape
    token_rows = student.shape[1]
    peers = 2 * LINE
    partner = {"vocab": v, "tokens": 1 - c}

    def slot_of(zs, ys, s):
        return (zs * 2 + ys) * 2 + (c + s - 2 * c * s)

    def rows_of(slot):
        return pl.ds(pl.multiple_of(slot * unit, unit), unit)

    def half(which):
        return pl.ds(pl.multiple_of(which * depth, 128), depth)

    own_slot = slot_of(z, y, 0)
    load_own = pltpu.make_async_copy(hidden.at[:, half(c)], feats.at[rows_of(own_slot)], load_sem.at[0])
    load_head = pltpu.make_async_copy(head, head_v, load_sem.at[1])
    load_student = pltpu.make_async_copy(student, student_v, load_sem.at[2])
    load_target = pltpu.make_async_copy(targets, target_v, load_sem.at[3])
    load_own.start()

    barrier = pltpu.get_barrier_semaphore()
    pl.semaphore_signal(barrier, inc=1, device_id=partner, device_id_type=MESH)
    for d in range(1, peers):
        peer = {"vocab": lax.rem(v + d, peers), "tokens": c}
        pl.semaphore_signal(barrier, inc=1, device_id=peer, device_id_type=MESH)
    pl.semaphore_wait(barrier, peers)

    def partner_copy():
        return pltpu.make_async_remote_copy(
            src_ref=hidden.at[:, half(1 - c)],
            dst_ref=feats.at[rows_of(own_slot)],
            send_sem=send_sem.at[3, own_slot],
            recv_sem=recv_sem.at[own_slot],
            device_id=partner,
            device_id_type=MESH,
        )

    def unit_copy(way, slot):
        target = (v + 2, v - 2, v + 1 - 2 * y)[way]
        return pltpu.make_async_remote_copy(
            src_ref=feats.at[rows_of(slot)],
            dst_ref=feats.at[rows_of(slot)],
            send_sem=send_sem.at[way, slot],
            recv_sem=recv_sem.at[slot],
            device_id={"vocab": target, "tokens": c},
            device_id_type=MESH,
        )

    def arrived(slot):
        unit_copy(2, slot).wait_recv()

    def send_line(way, slot):
        @pl.when(z < LINE - 1 if way == 0 else z > 0)
        def _():
            unit_copy(way, slot).start()

    def part_copy(block):
        return pltpu.make_async_remote_copy(
            src_ref=own_p.at[block],
            dst_ref=other_p.at[block],
            send_sem=part_send.at[block],
            recv_sem=part_recv.at[block],
            device_id=partner,
            device_id_type=MESH,
        )

    def multiply(block):
        rows = pl.ds(pl.multiple_of(block * 2 * unit, 2 * unit), 2 * unit)
        for first in range(0, cols, COLUMN_TILE):
            width = min(COLUMN_TILE, cols - first)
            own_p[block, first : first + width, :] = lax.dot_general(
                head_v[first : first + width, :],
                feats[rows, :],
                (((1,), (1,)), ((), ())),
                preferred_element_type=jnp.float32,
            )
        part_copy(block).start()

    partner_copy().start()
    load_own.wait()
    send_line(0, own_slot)
    send_line(1, own_slot)
    unit_copy(2, own_slot).start()
    load_head.start()
    load_student.start()
    load_target.start()
    own_second = slot_of(z, y, 1)
    arrived(own_second)
    send_line(0, own_second)
    send_line(1, own_second)
    unit_copy(2, own_second).start()

    load_student.wait()
    load_target.wait()
    entry = lax.broadcasted_iota(jnp.int32, (ROWS, 1), 0) + v * cols

    def rows8(values):
        return jnp.sum(values.reshape(-1, 8, values.shape[-1]), axis=0)

    sums_v[...] = jnp.zeros_like(sums_v)

    def student_pass(i, carry):
        rows = pl.ds(pl.multiple_of(i * ROWS, ROWS), ROWS)
        capped = capped_of(student_v[rows, :].astype(jnp.float32))
        grown = jnp.exp(capped)
        capped_v[rows, :] = capped
        exp_s[rows, :] = grown
        sums_v[0] += rows8(grown)
        sums_v[1] += rows8(jnp.where(target_v[...] == entry + i * ROWS, capped, 0.0))
        return carry

    passes = cols // ROWS
    load_head.wait()
    multiply(v)

    def step(k, carry):
        for s in range(2):
            src = z - 1 - k

            @pl.when(src >= 0)
            def _():
                slot = slot_of(src, y, s)
                arrived(slot)
                send_line(0, slot)

                @pl.when((src > 0) if s else (src >= 0))
                def _():
                    unit_copy(2, slot).start()

            src_up = z + 1 + k

            @pl.when(src_up <= LINE - 1)
            def _():
                slot = slot_of(src_up, y, s)
                arrived(slot)
                send_line(1, slot)

                @pl.when((src_up < LINE - 1) if s else (src_up <= LINE - 1))
                def _():
                    unit_copy(2, slot).start()

            if s == 0:
                @pl.when((z == k) & (z > 0))
                def _():
                    slot = slot_of(0, 1 - y, 1)
                    arrived(slot)
                    send_line(0, slot)

                @pl.when((LINE - 1 - z == k) & (z < LINE - 1))
                def _():
                    slot = slot_of(LINE - 1, 1 - y, 1)
                    arrived(slot)
                    send_line(1, slot)

            across = z - k

            @pl.when((across >= 0) & ((s == 0) | (across > 0) | (k == 0)))
            def _():
                slot = slot_of(across, 1 - y, s)
                arrived(slot)
                if s == 1:
                    @pl.when((k == 0) & (z == 0))
                    def _():
                        unit_copy(0, slot).start()

                    @pl.when((k == 0) & (z == LINE - 1))
                    def _():
                        unit_copy(1, slot).start()

            across_up = z + k

            @pl.when((k > 0) & (across_up <= LINE - 1) & ((s == 0) | (across_up < LINE - 1)))
            def _():
                arrived(slot_of(across_up, 1 - y, s))

        def products(which, inner):
            zs = jnp.where(which == 0, z - 1 - k, jnp.where(which == 1, z + 1 + k, jnp.where(which == 2, z - k, z + k)))
            ys = jnp.where(which < 2, y, 1 - y)

            @pl.when((zs >= 0) & (zs <= LINE - 1) & ((which < 3) | (k > 0)))
            def _():
                multiply(zs * 2 + ys)

            return inner

        lax.fori_loop(0, 4, products, 0)

        @pl.when(k < LINE - 1)
        def _():
            lax.fori_loop(k * passes // (LINE - 1), (k + 1) * passes // (LINE - 1), student_pass, 0)

        return carry

    lax.fori_loop(0, LINE, step, 0)

    def await_part(block, carry):
        part_copy(block).wait_recv()
        return carry

    lax.fori_loop(0, peers, await_part, 0)

    first_block = c * (token_rows // unit)
    lane = lax.broadcasted_iota(jnp.int32, (1, 2 * unit), 1)
    low = lane < unit
    tall = cols // 10
    for pair in range(token_rows // (2 * unit)):
        lanes = slice(pair * 2 * unit, (pair + 1) * 2 * unit)
        left = route[first_block + 2 * pair]
        right = route[first_block + 2 * pair + 1]
        left_at, right_at = left // 2, right // 2
        def teacher_pass(i, carry):
            total, cross = carry
            rows = pl.ds(pl.multiple_of(i * tall, 8), tall)
            one = own_p[left_at, rows, :] + other_p[left_at, rows, :]
            two = own_p[right_at, rows, :] + other_p[right_at, rows, :]
            placed = jnp.where(low, one, two)
            moved = pltpu.roll(jnp.where(low, two, one), unit, 1)
            teacher = capped_of(jnp.where(stay, placed, moved))
            grown = jnp.exp(teacher)
            exp_t[rows, lanes] = grown
            return total + rows8(grown), cross + rows8(grown * (teacher - capped_v[rows, lanes]))

        stay = jnp.where(low, left - 2 * left_at, 1 - (right - 2 * right_at)) == 0
        nothing = jnp.zeros((8, 2 * unit), jnp.float32)
        total, cross = lax.fori_loop(0, 10, teacher_pass, (nothing, nothing))
        sums_v[2, :, lanes] = total
        sums_v[3, :, lanes] = cross

    stat[...] = jnp.zeros_like(stat)
    for which in range(4):
        stat[which : which + 1, :] = jnp.sum(sums_v[which], axis=0, keepdims=True)

    def stat_copy(peer, slot):
        return pltpu.make_async_remote_copy(
            src_ref=stat,
            dst_ref=stat_all.at[slot],
            send_sem=stat_send.at[peer],
            recv_sem=stat_recv.at[slot],
            device_id={"vocab": peer, "tokens": c},
            device_id_type=MESH,
        )

    for d in range(1, peers):
        stat_copy(lax.rem(v + d, peers), v).start()
    stat_all[v] = stat[...]
    for d in range(1, peers):
        stat_copy(0, lax.rem(v + d, peers)).wait_recv()
    sums = stat_all[0]
    for d in range(1, peers):
        sums = sums + stat_all[d]
    log_student = jnp.log(sums[0:1, :])
    loss[...] = MIX_WEIGHT * (sums[3:4, :] / sums[2:3, :] - jnp.log(sums[2:3, :]) + log_student) + (
        1.0 - MIX_WEIGHT
    ) * (log_student - sums[1:2, :])
    student_scale = 1.0 / sums[0:1, :]
    teacher_scale = MIX_WEIGHT / sums[2:3, :]

    def gradient_pass(i, carry):
        rows = pl.ds(pl.multiple_of(i * ROWS, ROWS), ROWS)
        hits = jnp.where(target_v[...] == entry + i * ROWS, 1.0 - MIX_WEIGHT, 0.0)
        value = exp_s[rows, :] * student_scale - exp_t[rows, :] * teacher_scale - hits
        slope = 1.0 - (capped_v[rows, :] / SOFT_CAP) ** 2
        grad_v[rows, :] = (value * slope).astype(grad_v.dtype)
        return carry

    pieces = 5
    piece_rows = cols // pieces
    for p in range(pieces):
        lax.fori_loop(p * passes // pieces, (p + 1) * passes // pieces, gradient_pass, 0)
        rows = pl.ds(p * piece_rows, piece_rows)
        pltpu.make_async_copy(grad_v.at[rows], gradient.at[rows], store_sem.at[p]).start()

    partner_copy().wait_send()
    for s in range(2):
        def sent(zs, carry):
            slot = slot_of(zs, y, s)

            @pl.when((z < LINE - 1) & (zs <= z))
            def _():
                unit_copy(0, slot).wait_send()

            @pl.when((z > 0) & (zs >= z))
            def _():
                unit_copy(1, slot).wait_send()

            @pl.when((zs == z) | (s == 0) | ((zs > 0) & (zs < LINE - 1)))
            def _():
                unit_copy(2, slot).wait_send()

            return carry

        lax.fori_loop(0, LINE, sent, 0)

    @pl.when(z < LINE - 1)
    def _():
        unit_copy(0, slot_of(0, 1 - y, 1)).wait_send()

    @pl.when(z > 0)
    def _():
        unit_copy(1, slot_of(LINE - 1, 1 - y, 1)).wait_send()

    def sent_part(block, carry):
        part_copy(block).wait_send()
        return carry

    lax.fori_loop(0, peers, sent_part, 0)
    for d in range(1, peers):
        stat_copy(lax.rem(v + d, peers), v).wait_send()
    for p in range(pieces):
        rows = pl.ds(p * piece_rows, piece_rows)
        pltpu.make_async_copy(grad_v.at[rows], gradient.at[rows], store_sem.at[p]).wait()


def fused(teacher_hidden, route, teacher_head, student_logits, targets):
    tokens, cols = student_logits.shape
    depth = teacher_head.shape[0]
    unit = teacher_hidden.shape[0]
    units = 4 * LINE
    anywhere = pl.BlockSpec(memory_space=pl.ANY)
    dma = pltpu.SemaphoreType.DMA
    gradient, loss = pl.pallas_call(
        fused_kernel,
        out_shape=(
            jax.ShapeDtypeStruct((cols, tokens), jnp.bfloat16),
            jax.ShapeDtypeStruct((1, tokens), jnp.float32),
        ),
        in_specs=[anywhere, pl.BlockSpec(memory_space=pltpu.SMEM), anywhere, anywhere, anywhere],
        out_specs=(anywhere, pl.BlockSpec(memory_space=pltpu.VMEM)),
        scratch_shapes=[
            pltpu.VMEM((cols, depth), jnp.bfloat16),
            pltpu.VMEM((units * unit, depth), jnp.bfloat16),
            pltpu.VMEM((units // 2, cols, 2 * unit), jnp.float32),
            pltpu.VMEM((units // 2, cols, 2 * unit), jnp.float32),
            pltpu.VMEM((cols, tokens), jnp.bfloat16),
            pltpu.VMEM((cols, tokens), jnp.float32),
            pltpu.VMEM((cols, tokens), jnp.float32),
            pltpu.VMEM((cols, tokens), jnp.float32),
            pltpu.VMEM((cols, tokens), jnp.bfloat16),
            pltpu.VMEM((1, tokens), jnp.int32),
            pltpu.VMEM((8, tokens), jnp.float32),
            pltpu.VMEM((2 * LINE, 8, tokens), jnp.float32),
            pltpu.VMEM((4, 8, tokens), jnp.float32),
            dma((4,)),
            dma((4, units)),
            dma((units,)),
            dma((2 * LINE,)),
            dma((2 * LINE,)),
            dma((2 * LINE,)),
            dma((2 * LINE,)),
            dma((5,)),
        ],
        compiler_params=pltpu.CompilerParams(
            collective_id=0, has_side_effects=True, vmem_limit_bytes=56 * 2**20
        ),
    )(teacher_hidden, route, teacher_head.T, student_logits.T, targets[None, :])
    return gradient.T, loss.reshape(tokens)


def solution(mesh):
    body = fused if mesh.shape["vocab"] == 2 * LINE else per_device
    return jax.shard_map(
        body,
        mesh=mesh,
        in_specs=(
            P(("groups", "vocab", "tokens"), None),
            P("groups"),
            P("tokens", "vocab"),
            P(("groups", "tokens"), "vocab"),
            P(("groups", "tokens")),
        ),
        out_specs=(P(("groups", "tokens"), "vocab"), P(("groups", "tokens"))),
        check_vma=False,
    )
```

```python
import jax
import jax.numpy as jnp
from jax import lax
from jax.experimental import pallas as pl
from jax.experimental.pallas import tpu as pltpu
from jax.sharding import PartitionSpec as P

BLOCK_ROWS = 64


SOFT_CAP = 30.0
MIX_WEIGHT = 0.5


def from_partner(value, axis, bit):
    mask = 2**bit
    pairs = [(source, source ^ mask) for source in range(lax.axis_size(axis))]
    return lax.ppermute(value, axis, pairs)


def capped_of(values):
    return SOFT_CAP * jnp.tanh(values / SOFT_CAP)


def logit_terms(features, weights):
    return jnp.dot(features, weights, preferred_element_type=jnp.float32)


def per_device(teacher_hidden, route, teacher_head, student_logits, targets):
    row_count, col_count = student_logits.shape
    head_rows = teacher_head.shape[0]
    token_index = lax.axis_index("tokens")
    vocab_index = lax.axis_index("vocab")
    capped = capped_of(student_logits.astype(jnp.float32))
    exp_student = jnp.exp(capped)
    columns = vocab_index * col_count + lax.broadcasted_iota(jnp.int32, (1, col_count), 1)
    target_hits = targets[:, None] == columns
    picked_part = jnp.sum(jnp.where(target_hits, capped, 0.0), axis=1)
    student_part = jnp.sum(exp_student, axis=1)
    own_half = lax.dynamic_slice_in_dim(teacher_hidden, token_index * head_rows, head_rows, 1)
    given_half = lax.dynamic_slice_in_dim(
        teacher_hidden, (1 - token_index) * head_rows, head_rows, 1
    )
    received = from_partner(given_half, "tokens", 0)
    lower_rows = jnp.where(token_index == 0, own_half, received)
    upper_rows = jnp.where(token_index == 0, received, own_half)
    paired = jnp.concatenate((lower_rows, upper_rows), axis=0)
    sliced = lax.all_gather(paired, "vocab", axis=0, tiled=True)
    half_blocks = sliced.reshape(-1, BLOCK_ROWS, head_rows)
    features = jnp.take(half_blocks, route, axis=0).reshape(-1, head_rows)
    teacher_raw = lax.psum_scatter(
        logit_terms(features, teacher_head), "tokens", scatter_dimension=0, tiled=True
    )
    teacher_capped = capped_of(teacher_raw)
    exp_teacher = jnp.exp(teacher_capped)
    teacher_part = jnp.sum(exp_teacher, axis=1)
    cross_part = jnp.sum(exp_teacher * (teacher_capped - capped), axis=1)
    student_total, picked, teacher_total, cross_sum = lax.psum(
        (student_part, picked_part, teacher_part, cross_part), "vocab"
    )
    log_student = jnp.log(student_total)
    token_loss = MIX_WEIGHT * (cross_sum / teacher_total - jnp.log(teacher_total) + log_student) + (
        1.0 - MIX_WEIGHT
    ) * (log_student - picked)
    cap_slope = 1.0 - (capped / SOFT_CAP) ** 2
    gradient = (
        exp_student / student_total[:, None]
        - MIX_WEIGHT * exp_teacher / teacher_total[:, None]
        - (1.0 - MIX_WEIGHT) * target_hits.astype(jnp.float32)
    ) * cap_slope
    return (gradient.astype(jnp.bfloat16), token_loss)


MESH = pl.DeviceIdType.MESH
ROWS = 80
LINE = 4
COLUMN_TILE = 400


def fused_kernel(
    hidden, route, head, student, targets,
    gradient, loss,
    head_v, feats, own_p, other_p, student_v, capped_v, exp_s, exp_t, grad_v, target_v,
    stat, stat_all, sums_v,
    load_sem, send_sem, recv_sem, part_send, part_recv, stat_send, stat_recv, store_sem,
):
    c = lax.axis_index("tokens")
    v = lax.axis_index("vocab")
    z = v // 2
    y = v - 2 * z
    unit = hidden.shape[0]
    cols, depth = head.shape
    token_rows = student.shape[1]
    peers = 2 * LINE
    partner = {"vocab": v, "tokens": 1 - c}

    def slot_of(zs, ys, s):
        return (zs * 2 + ys) * 2 + (c + s - 2 * c * s)

    def rows_of(slot):
        return pl.ds(pl.multiple_of(slot * unit, unit), unit)

    def half(which):
        return pl.ds(pl.multiple_of(which * depth, 128), depth)

    own_slot = slot_of(z, y, 0)
    load_own = pltpu.make_async_copy(hidden.at[:, half(c)], feats.at[rows_of(own_slot)], load_sem.at[0])
    load_head = pltpu.make_async_copy(head, head_v, load_sem.at[1])
    load_student = pltpu.make_async_copy(student, student_v, load_sem.at[2])
    load_target = pltpu.make_async_copy(targets, target_v, load_sem.at[3])
    load_own.start()
    load_head.start()
    load_student.start()
    load_target.start()

    barrier = pltpu.get_barrier_semaphore()
    pl.semaphore_signal(barrier, inc=1, device_id=partner, device_id_type=MESH)
    for d in range(1, peers):
        peer = {"vocab": lax.rem(v + d, peers), "tokens": c}
        pl.semaphore_signal(barrier, inc=1, device_id=peer, device_id_type=MESH)
    pl.semaphore_wait(barrier, peers)

    def partner_copy():
        return pltpu.make_async_remote_copy(
            src_ref=hidden.at[:, half(1 - c)],
            dst_ref=feats.at[rows_of(own_slot)],
            send_sem=send_sem.at[3, own_slot],
            recv_sem=recv_sem.at[own_slot],
            device_id=partner,
            device_id_type=MESH,
        )

    def unit_copy(way, slot):
        target = (v + 2, v - 2, v + 1 - 2 * y)[way]
        return pltpu.make_async_remote_copy(
            src_ref=feats.at[rows_of(slot)],
            dst_ref=feats.at[rows_of(slot)],
            send_sem=send_sem.at[way, slot],
            recv_sem=recv_sem.at[slot],
            device_id={"vocab": target, "tokens": c},
            device_id_type=MESH,
        )

    def arrived(slot):
        unit_copy(2, slot).wait_recv()

    def send_line(way, slot):
        @pl.when(z < LINE - 1 if way == 0 else z > 0)
        def _():
            unit_copy(way, slot).start()

    def part_copy(block):
        return pltpu.make_async_remote_copy(
            src_ref=own_p.at[block],
            dst_ref=other_p.at[block],
            send_sem=part_send.at[block],
            recv_sem=part_recv.at[block],
            device_id=partner,
            device_id_type=MESH,
        )

    def multiply(block):
        rows = pl.ds(pl.multiple_of(block * 2 * unit, 2 * unit), 2 * unit)
        for first in range(0, cols, COLUMN_TILE):
            width = min(COLUMN_TILE, cols - first)
            own_p[block, first : first + width, :] = lax.dot_general(
                head_v[first : first + width, :],
                feats[rows, :],
                (((1,), (1,)), ((), ())),
                preferred_element_type=jnp.float32,
            )
        part_copy(block).start()

    partner_copy().start()
    load_own.wait()
    send_line(0, own_slot)
    send_line(1, own_slot)
    unit_copy(2, own_slot).start()
    own_second = slot_of(z, y, 1)
    arrived(own_second)
    send_line(0, own_second)
    send_line(1, own_second)
    unit_copy(2, own_second).start()

    load_student.wait()
    load_target.wait()
    entry = lax.broadcasted_iota(jnp.int32, (ROWS, 1), 0) + v * cols

    def rows8(values):
        return jnp.sum(values.reshape(-1, 8, values.shape[-1]), axis=0)

    sums_v[...] = jnp.zeros_like(sums_v)

    def student_pass(i, carry):
        rows = pl.ds(pl.multiple_of(i * ROWS, ROWS), ROWS)
        capped = capped_of(student_v[rows, :].astype(jnp.float32))
        grown = jnp.exp(capped)
        capped_v[rows, :] = capped
        exp_s[rows, :] = grown
        sums_v[0] += rows8(grown)
        sums_v[1] += rows8(jnp.where(target_v[...] == entry + i * ROWS, capped, 0.0))
        return carry

    passes = cols // ROWS
    load_head.wait()
    multiply(v)

    def step(k, carry):
        for s in range(2):
            src = z - 1 - k

            @pl.when(src >= 0)
            def _():
                slot = slot_of(src, y, s)
                arrived(slot)
                send_line(0, slot)

                @pl.when((src > 0) if s else (src >= 0))
                def _():
                    unit_copy(2, slot).start()

            src_up = z + 1 + k

            @pl.when(src_up <= LINE - 1)
            def _():
                slot = slot_of(src_up, y, s)
                arrived(slot)
                send_line(1, slot)

                @pl.when((src_up < LINE - 1) if s else (src_up <= LINE - 1))
                def _():
                    unit_copy(2, slot).start()

            if s == 0:
                @pl.when((z == k) & (z > 0))
                def _():
                    slot = slot_of(0, 1 - y, 1)
                    arrived(slot)
                    send_line(0, slot)

                @pl.when((LINE - 1 - z == k) & (z < LINE - 1))
                def _():
                    slot = slot_of(LINE - 1, 1 - y, 1)
                    arrived(slot)
                    send_line(1, slot)

            across = z - k

            @pl.when((across >= 0) & ((s == 0) | (across > 0) | (k == 0)))
            def _():
                slot = slot_of(across, 1 - y, s)
                arrived(slot)
                if s == 1:
                    @pl.when((k == 0) & (z == 0))
                    def _():
                        unit_copy(0, slot).start()

                    @pl.when((k == 0) & (z == LINE - 1))
                    def _():
                        unit_copy(1, slot).start()

            across_up = z + k

            @pl.when((k > 0) & (across_up <= LINE - 1) & ((s == 0) | (across_up < LINE - 1)))
            def _():
                arrived(slot_of(across_up, 1 - y, s))

            if s == 0:
                @pl.when(k < LINE - 1)
                def _():
                    lax.fori_loop(k * passes // (LINE - 1), (k + 1) * passes // (LINE - 1), student_pass, 0)

        def products(which, inner):
            zs = jnp.where(which == 0, z - 1 - k, jnp.where(which == 1, z + 1 + k, jnp.where(which == 2, z - k, z + k)))
            ys = jnp.where(which < 2, y, 1 - y)

            @pl.when((zs >= 0) & (zs <= LINE - 1) & ((which < 3) | (k > 0)))
            def _():
                multiply(zs * 2 + ys)

            return inner

        lax.fori_loop(0, 4, products, 0)

        return carry

    lax.fori_loop(0, LINE, step, 0)

    def await_part(block, carry):
        part_copy(block).wait_recv()
        return carry

    lax.fori_loop(0, peers, await_part, 0)

    first_block = c * (token_rows // unit)
    lane = lax.broadcasted_iota(jnp.int32, (1, 2 * unit), 1)
    low = lane < unit
    tall = cols // 10
    for pair in range(token_rows // (2 * unit)):
        lanes = slice(pair * 2 * unit, (pair + 1) * 2 * unit)
        left = route[first_block + 2 * pair]
        right = route[first_block + 2 * pair + 1]
        left_at, right_at = left // 2, right // 2
        def teacher_pass(i, carry):
            total, cross = carry
            rows = pl.ds(pl.multiple_of(i * tall, 8), tall)
            one = own_p[left_at, rows, :] + other_p[left_at, rows, :]
            two = own_p[right_at, rows, :] + other_p[right_at, rows, :]
            placed = jnp.where(low, one, two)
            moved = pltpu.roll(jnp.where(low, two, one), unit, 1)
            teacher = capped_of(jnp.where(stay, placed, moved))
            grown = jnp.exp(teacher)
            exp_t[rows, lanes] = grown
            return total + rows8(grown), cross + rows8(grown * (teacher - capped_v[rows, lanes]))

        stay = jnp.where(low, left - 2 * left_at, 1 - (right - 2 * right_at)) == 0
        nothing = jnp.zeros((8, 2 * unit), jnp.float32)
        total, cross = lax.fori_loop(0, 10, teacher_pass, (nothing, nothing))
        sums_v[2, :, lanes] = total
        sums_v[3, :, lanes] = cross

    stat[...] = jnp.zeros_like(stat)
    for which in range(4):
        stat[which : which + 1, :] = jnp.sum(sums_v[which], axis=0, keepdims=True)

    def stat_copy(peer, slot):
        return pltpu.make_async_remote_copy(
            src_ref=stat,
            dst_ref=stat_all.at[slot],
            send_sem=stat_send.at[peer],
            recv_sem=stat_recv.at[slot],
            device_id={"vocab": peer, "tokens": c},
            device_id_type=MESH,
        )

    for d in range(1, peers):
        stat_copy(lax.rem(v + d, peers), v).start()
    stat_all[v] = stat[...]
    for d in range(1, peers):
        stat_copy(0, lax.rem(v + d, peers)).wait_recv()
    sums = stat_all[0]
    for d in range(1, peers):
        sums = sums + stat_all[d]
    log_student = jnp.log(sums[0:1, :])
    loss[...] = MIX_WEIGHT * (sums[3:4, :] / sums[2:3, :] - jnp.log(sums[2:3, :]) + log_student) + (
        1.0 - MIX_WEIGHT
    ) * (log_student - sums[1:2, :])
    student_scale = 1.0 / sums[0:1, :]
    teacher_scale = MIX_WEIGHT / sums[2:3, :]

    def gradient_pass(i, carry):
        rows = pl.ds(pl.multiple_of(i * ROWS, ROWS), ROWS)
        hits = jnp.where(target_v[...] == entry + i * ROWS, 1.0 - MIX_WEIGHT, 0.0)
        value = exp_s[rows, :] * student_scale - exp_t[rows, :] * teacher_scale - hits
        slope = 1.0 - (capped_v[rows, :] / SOFT_CAP) ** 2
        grad_v[rows, :] = (value * slope).astype(grad_v.dtype)
        return carry

    pieces = 5
    piece_rows = cols // pieces
    for p in range(pieces):
        lax.fori_loop(p * passes // pieces, (p + 1) * passes // pieces, gradient_pass, 0)
        rows = pl.ds(p * piece_rows, piece_rows)
        pltpu.make_async_copy(grad_v.at[rows], gradient.at[rows], store_sem.at[p]).start()

    partner_copy().wait_send()
    for s in range(2):
        def sent(zs, carry):
            slot = slot_of(zs, y, s)

            @pl.when((z < LINE - 1) & (zs <= z))
            def _():
                unit_copy(0, slot).wait_send()

            @pl.when((z > 0) & (zs >= z))
            def _():
                unit_copy(1, slot).wait_send()

            @pl.when((zs == z) | (s == 0) | ((zs > 0) & (zs < LINE - 1)))
            def _():
                unit_copy(2, slot).wait_send()

            return carry

        lax.fori_loop(0, LINE, sent, 0)

    @pl.when(z < LINE - 1)
    def _():
        unit_copy(0, slot_of(0, 1 - y, 1)).wait_send()

    @pl.when(z > 0)
    def _():
        unit_copy(1, slot_of(LINE - 1, 1 - y, 1)).wait_send()

    def sent_part(block, carry):
        part_copy(block).wait_send()
        return carry

    lax.fori_loop(0, peers, sent_part, 0)
    for d in range(1, peers):
        stat_copy(lax.rem(v + d, peers), v).wait_send()
    for p in range(pieces):
        rows = pl.ds(p * piece_rows, piece_rows)
        pltpu.make_async_copy(grad_v.at[rows], gradient.at[rows], store_sem.at[p]).wait()


def fused(teacher_hidden, route, teacher_head, student_logits, targets):
    tokens, cols = student_logits.shape
    depth = teacher_head.shape[0]
    unit = teacher_hidden.shape[0]
    units = 4 * LINE
    anywhere = pl.BlockSpec(memory_space=pl.ANY)
    dma = pltpu.SemaphoreType.DMA
    gradient, loss = pl.pallas_call(
        fused_kernel,
        out_shape=(
            jax.ShapeDtypeStruct((cols, tokens), jnp.bfloat16),
            jax.ShapeDtypeStruct((1, tokens), jnp.float32),
        ),
        in_specs=[anywhere, pl.BlockSpec(memory_space=pltpu.SMEM), anywhere, anywhere, anywhere],
        out_specs=(anywhere, pl.BlockSpec(memory_space=pltpu.VMEM)),
        scratch_shapes=[
            pltpu.VMEM((cols, depth), jnp.bfloat16),
            pltpu.VMEM((units * unit, depth), jnp.bfloat16),
            pltpu.VMEM((units // 2, cols, 2 * unit), jnp.float32),
            pltpu.VMEM((units // 2, cols, 2 * unit), jnp.float32),
            pltpu.VMEM((cols, tokens), jnp.bfloat16),
            pltpu.VMEM((cols, tokens), jnp.float32),
            pltpu.VMEM((cols, tokens), jnp.float32),
            pltpu.VMEM((cols, tokens), jnp.float32),
            pltpu.VMEM((cols, tokens), jnp.bfloat16),
            pltpu.VMEM((1, tokens), jnp.int32),
            pltpu.VMEM((8, tokens), jnp.float32),
            pltpu.VMEM((2 * LINE, 8, tokens), jnp.float32),
            pltpu.VMEM((4, 8, tokens), jnp.float32),
            dma((4,)),
            dma((4, units)),
            dma((units,)),
            dma((2 * LINE,)),
            dma((2 * LINE,)),
            dma((2 * LINE,)),
            dma((2 * LINE,)),
            dma((5,)),
        ],
        compiler_params=pltpu.CompilerParams(
            collective_id=0, has_side_effects=True, vmem_limit_bytes=56 * 2**20
        ),
    )(teacher_hidden, route, teacher_head.T, student_logits.T, targets[None, :])
    return gradient.T, loss.reshape(tokens)


def solution(mesh):
    body = fused if mesh.shape["vocab"] == 2 * LINE else per_device
    return jax.shard_map(
        body,
        mesh=mesh,
        in_specs=(
            P(("groups", "vocab", "tokens"), None),
            P("groups"),
            P("tokens", "vocab"),
            P(("groups", "tokens"), "vocab"),
            P(("groups", "tokens")),
        ),
        out_specs=(P(("groups", "tokens"), "vocab"), P(("groups", "tokens"))),
        check_vma=False,
    )
```
